128 devices in a mesh: tile: 32 (over x, y, core), mem: 4 (over z).
Axes of the slice: x: 4, y: 4, z: 4, core: 2. Of those that a mesh axis runs over, the one named last changes fastest.
Arguments:
- control: bfloat16 [80, 1, 1440, 720], P('mem', None, 'tile'), may hold values from -6 to 6
- perturb: bfloat16 [80, 1, 1440, 720], P('mem', None, 'tile'), may hold values from -6 to 6
- lon_taps: bfloat16 [17], replicated, may hold values from 0.026367188 to 0.07910156
- lat_taps: bfloat16 [17], replicated, may hold values from 0.026367188 to 0.07910156
- innov: float32 [32, 32, 256], P('tile'), may hold values from -6 to 6
- inv_var: float32 [32, 32, 256], P('tile'), may hold values from 1 to 8
- cell_index: int32 [32, 32, 256], P('tile'), may hold values from 0 to 32399, as said below
- counts: int32 [32, 32], P('tile'), may hold values from 0 to 256, as said below
Outputs:
- gradient: float32 [80, 1, 1440, 720], P('mem', None, 'tile')
The draws below stay inside these ranges and needn't reach their ends.
Inputs may be any that keep to these rules, and one draw needn't show every extreme that they name: `cell_index`: an observation's cell within its owning tile, level * 45 * 720 + longitude within the tile * 720 + latitude; both ends are taken. `counts`: live slots per pair of tiles; some pair fills all 256 slots in every draw, and some owning tiles receive far more than others.
All inputs are finite; a program needn't handle non-finite values.
Results may differ from the reference program's by a relative error of at most 0.00066.
Values may be sent and summed in bfloat16 or wider, within the bound.
A program may use at most 64 MiB of HBM per device.

```python
import math
import jax
import jax.numpy as jnp
from jax import lax

LEV = 1
LON_DEV = 45
LAT = 720
RAD = 16
CAP = 256
TILES = 32
LON = 1440
MEMBERS = 80
CELLS = 32400


def draw_cell_index(key, part):
    total_cells = LEV * LON_DEV * LAT
    drawn = jax.random.randint(key, (TILES, TILES, CAP), 0, total_cells, dtype=jnp.int32)
    drawn = drawn.at[0, 0, 0].set(0)
    return drawn.at[TILES - 1, TILES - 1, CAP - 1].set(total_cells - 1)


def draw_counts(key, part):
    raw_key = jax.random.fold_in(key, 11)
    level_key = jax.random.fold_in(key, 12)
    source_key = jax.random.fold_in(key, 13)
    target_key = jax.random.fold_in(key, 14)
    raw_counts = jax.random.randint(raw_key, (TILES, TILES), 0, CAP + 1, dtype=jnp.int32)
    levels_drawn = jax.random.randint(level_key, (TILES,), 0, 4, dtype=jnp.int32)
    density = jnp.array([1, 2, 4, 8], dtype=jnp.int32)[levels_drawn]
    scaled = jnp.minimum(raw_counts * density[None, :] // 4, CAP)
    heavy_source = jax.random.randint(source_key, (), 0, TILES, dtype=jnp.int32)
    heavy_target = jax.random.randint(target_key, (), 0, TILES, dtype=jnp.int32)
    return scaled.at[heavy_source, heavy_target].set(CAP)


def level_of(own_key, extent, shards, smallest, top_value):
    level, own = 1.0, jax.random.fold_in(own_key, 6)
    for dim, shards_of in shards:
        heights = jnp.exp(jax.random.uniform(jax.random.fold_in(own, dim), (shards_of,), jnp.float32, smallest / len(shards), top_value / len(shards)))
        level = level * jnp.repeat(heights, extent[dim] // shards_of).reshape([-1 if axis == dim else 1 for axis in range(len(extent))])
    return level


def gaussian(rng, extent, scale, reach, split=(), kind=jnp.bfloat16):
    values = jax.random.normal(rng, extent, jnp.float32) * scale
    if len(split) > 0:
        values = level_of(rng, extent, split, -0.22, 0.18) * values
    return jnp.clip(values, min=-reach, max=reach).astype(kind)


def setup_inputs(seed: int = 0) -> dict:
    key_of = jax.random.split(jax.random.key(seed), 9)
    control = gaussian(key_of[0], (MEMBERS, LEV, LON, LAT), 1.0, 6.0, ((0, 4), (2, 32)))
    perturb = gaussian(key_of[1], (MEMBERS, LEV, LON, LAT), 1.0, 6.0, ((0, 4), (2, 32)))
    lon_taps = jnp.clip(jax.random.uniform(key_of[2], (RAD + 1,), jnp.float32, 0.026367188, 0.07910156), 0.026367188, 0.07910156).astype(jnp.bfloat16)
    lat_taps = jnp.clip(jax.random.uniform(key_of[3], (RAD + 1,), jnp.float32, 0.026367188, 0.07910156), 0.026367188, 0.07910156).astype(jnp.bfloat16)
    innov = gaussian(key_of[4], (TILES, TILES, CAP), 1.0, 6.0, ((0, 32),), jnp.float32)
    inv_var = jnp.clip(jnp.exp(math.log(8.0) - 2.0794415 * jax.random.uniform(key_of[5], (TILES, TILES, CAP), jnp.float32) ** level_of(key_of[5], (TILES, TILES, CAP), ((0, 32),), -0.2, 0.2)), 1.0, 8.0)
    cell_index = draw_cell_index(jax.random.fold_in(key_of[8], 71), 0)
    counts = draw_counts(jax.random.fold_in(key_of[8], 71), 0)
    return dict(control=control, perturb=perturb, lon_taps=lon_taps, lat_taps=lat_taps, innov=innov, inv_var=inv_var, cell_index=cell_index, counts=counts)


def along_lon(grid_field, tap_weights):
    taps = tap_weights.astype(jnp.float32)
    field = grid_field.astype(jnp.float32)
    result = taps[0] * field
    for offset in range(1, RAD + 1):
        result = result + taps[offset] * (jnp.roll(field, offset, axis=-2) + jnp.roll(field, -offset, axis=-2))
    return result.astype(jnp.bfloat16)


def along_lat(grid_field, tap_weights):
    taps = tap_weights.astype(jnp.float32)
    field = grid_field.astype(jnp.float32)
    padded = jnp.pad(field, ((0, 0), (0, 0), (RAD, RAD)))
    result = taps[0] * field
    for offset in range(1, RAD + 1):
        result = result + taps[offset] * (padded[:, :, RAD + offset:RAD + offset + LAT] + padded[:, :, RAD - offset:RAD - offset + LAT])
    return result


def reference(control, perturb, lon_taps, lat_taps, innov, inv_var, cell_index, counts):
    def forward(running, member_pair):
        member, member_pert = member_pair
        smoothed = along_lat(along_lon(member, lon_taps), lat_taps)
        return running + member_pert.astype(jnp.float32) * smoothed, None

    increment, _ = lax.scan(forward, jnp.zeros((LEV, LON, LAT), jnp.float32), (control, perturb))
    by_tile = increment.reshape(LEV, TILES, LON_DEV, LAT).transpose(1, 0, 2, 3).reshape(TILES, CELLS)
    targets = cell_index.transpose(1, 0, 2).reshape(TILES, TILES * CAP).astype(jnp.int32)
    slot_ids = jnp.arange(CAP, dtype=jnp.int32)
    is_live = slot_ids[None, None, :] < counts[:, :, None]
    weights = jnp.where(is_live, inv_var, jnp.zeros_like(inv_var)).transpose(1, 0, 2).reshape(TILES, TILES * CAP)
    observed = innov.transpose(1, 0, 2).reshape(TILES, TILES * CAP)
    picked = jnp.take_along_axis(by_tile, targets, axis=1)
    misfit = weights * (picked - observed)

    def spread_tile(values, positions):
        return jnp.zeros((CELLS,), misfit.dtype).at[positions].add(values)

    spread = jax.vmap(spread_tile)(misfit, targets)
    spread = spread.reshape(TILES, LEV, LON_DEV, LAT).transpose(1, 0, 2, 3).reshape(LEV, LON, LAT)

    def backward(member_pair):
        member, member_pert = member_pair
        weighted = (member_pert.astype(jnp.float32) * spread).astype(jnp.bfloat16)
        return member.astype(jnp.float32) + along_lat(along_lon(weighted, lon_taps), lat_taps)

    return lax.map(backward, (control, perturb))
```

```python
import functools

import jax
import jax.numpy as jnp
from jax import lax
from jax.experimental import pallas as pl
from jax.experimental.pallas import tpu as pltpu
from jax.sharding import PartitionSpec as P

MESH = pl.DeviceIdType.MESH
F32 = jnp.float32
BF16 = jnp.bfloat16
SUM_TYPE = jnp.float32
GROUP = 5


def tap_columns(taps_ref):
    row = taps_ref[...].astype(F32).reshape(1, -1)
    return [row[:, d : d + 1] for d in range(row.shape[1])]


def band_of(distance, taps):
    band = jnp.zeros(distance.shape, F32)
    for d, tap in enumerate(taps):
        band = jnp.where(distance == d, tap, band)
    return band


def iota(shape, dim):
    return lax.broadcasted_iota(jnp.int32, shape, dim)


def build_bands(lon_ref, lat_ref, own_band, side_band, lat_band):
    lon_taps = tap_columns(lon_ref)
    lat_taps = tap_columns(lat_ref)
    rad = len(lon_taps) - 1
    shape = own_band.shape
    own_band[...] = band_of(jnp.abs(iota(shape, 0) - iota(shape, 1)), lon_taps).astype(BF16)
    shape = side_band.shape
    rows, cols = iota(shape, 0), iota(shape, 1)
    lon_cells = own_band.shape[1]
    place = jnp.where(cols < rad, cols - rad, cols - rad + lon_cells)
    side_band[...] = band_of(jnp.abs(rows - place), lon_taps).astype(BF16)
    width = lat_band.shape[1]

    def fill(i, carry):
        shape = (16, width)
        start = pl.multiple_of(i * 16, 16)
        away = jnp.abs(iota(shape, 0) + (start - 128) - iota(shape, 1))
        lat_band[pl.ds(start, 16), :] = band_of(away, lat_taps).astype(BF16)
        return carry

    lax.fori_loop(0, lat_band.shape[0] // 16, fill, 0)


def dot(a, b):
    return jnp.dot(a, b, preferred_element_type=F32)


def along_lat(field, band, out):
    lat = field.shape[1]
    out[:, 0:256] = dot(field[:, 0:384], band[128:512, :])
    out[:, 256:512] = dot(field[:, 128:640], band[0:512, :])
    out[:, 512:lat] = dot(field[:, 384:lat], band[0 : lat - 384, 0 : lat - 512])


def forward_kernel(
    tiles,
    groups,
    control,
    perturb,
    lon_taps,
    lat_taps,
    innov,
    inv_var,
    cell_index,
    counts,
    spread_own,
    spread_side,
    perturb_side,
    own_band,
    side_band,
    lat_band,
    control_own,
    perturb_own,
    control_low,
    perturb_low,
    control_side,
    along,
    smooth,
    total,
    send_sum,
    send_edge,
    got_sum,
    got_edge,
    lists,
    stage,
    got_lists,
    onehot,
    picked,
    places,
    field_parts,
    fields,
    field_edge,
    got_field,
    load_sem,
    halo_send,
    halo_recv,
    list_send,
    list_recv,
    sum_send,
    sum_recv,
    edge_send,
    edge_recv,
    field_send,
    field_recv,
):
    me = lax.axis_index("tile")
    mine = lax.axis_index("mem")
    mems = got_sum.shape[0] + 1
    members, lon_cells, lat = control_own.shape
    rad = control_side.shape[1] // 2
    cap = innov.shape[2]
    left, right = lax.rem(me + tiles - 1, tiles), lax.rem(me + 1, tiles)
    sides = (left, right)

    loads = [
        pltpu.make_async_copy(
            control.at[pl.ds(g * GROUP, GROUP), 0],
            control_own.at[pl.ds(g * GROUP, GROUP)],
            load_sem.at[g],
        )
        for g in range(groups)
    ]
    loads.append(pltpu.make_async_copy(perturb.at[:, 0], perturb_own, load_sem.at[groups]))
    loads.append(pltpu.make_async_copy(inv_var.at[0], lists.at[0], load_sem.at[groups + 1]))
    loads.append(pltpu.make_async_copy(innov.at[0], lists.at[1], load_sem.at[groups + 2]))
    for load in loads:
        load.start()

    partners = [(tile, mine) for tile in sides]
    partners += [(me, lax.rem(mine + j, mems)) for j in range(1, mems)]
    partners += [(tile, lax.rem(mine + j, mems)) for tile in sides for j in range(1, mems)]
    partners += [(lax.rem(me + i, tiles), mine) for i in range(2, tiles - 1)]
    barrier = pltpu.get_barrier_semaphore()
    for partner in partners:
        pl.semaphore_signal(barrier, inc=1, device_id=partner, device_id_type=MESH)

    def low_edge(own, low, start):
        for k in range(GROUP):
            field = own[start + k].astype(F32)
            low[start + k] = field[lon_cells - rad :, :].astype(BF16)

    for g in range(groups):
        loads[g].wait()
        low_edge(control_own, control_low, g * GROUP)

    def list_copy(i):
        return pltpu.make_async_remote_copy(
            stage.at[lax.rem(me + i, tiles)],
            got_lists.at[i],
            list_send.at[i],
            list_recv.at[i],
            device_id=(lax.rem(me + i, tiles), mine),
            device_id_type=MESH,
        )

    def halo_copies(own, low, side, kind, g):
        chunk = pl.ds(g * GROUP, GROUP)
        return (
            pltpu.make_async_remote_copy(
                own.at[chunk, 0:rad],
                side.at[chunk, rad : 2 * rad],
                halo_send.at[kind, 0, g],
                halo_recv.at[kind, 0, g],
                device_id=(left, mine),
                device_id_type=MESH,
            ),
            pltpu.make_async_remote_copy(
                low.at[chunk],
                side.at[chunk, 0:rad],
                halo_send.at[kind, 1, g],
                halo_recv.at[kind, 1, g],
                device_id=(right, mine),
                device_id_type=MESH,
            ),
        )

    def control_copies(g):
        return halo_copies(control_own, control_low, control_side, 0, g)

    def perturb_copies(g):
        return halo_copies(perturb_own, perturb_low, perturb_side, 1, g)

    pl.semaphore_wait(barrier, len(partners))
    for g in range(groups):
        for copy in control_copies(g):
            copy.start()

    for load in loads[groups:]:
        load.wait()
    shape = (tiles, tiles)
    count_row = counts[...].astype(F32)
    count_col = jnp.sum(
        jnp.where(iota(shape, 0) == iota(shape, 1), count_row, 0.0), axis=1, keepdims=True
    )
    live = iota((tiles, cap), 1).astype(F32) < count_col
    weight = jnp.where(live, lists[0], 0.0)
    stage[:, 0, 0:cap] = weight
    stage[:, 0, cap : 2 * cap] = weight * lists[1]
    stage[:, 0, 2 * cap : 3 * cap] = cell_index[0].astype(F32)
    for i in range(1, tiles):
        list_copy(i).start()
    got_lists[0] = stage[me]
    for g in range(groups):
        low_edge(perturb_own, perturb_low, g * GROUP)
    build_bands(lon_taps, lat_taps, own_band, side_band, lat_band)

    total[...] = jnp.zeros_like(total)
    rows = own_band.shape[0]

    def forward(g, carry):
        for copy in control_copies(g):
            copy.wait_recv()
        for copy in perturb_copies(g):
            copy.start()
        for k in range(GROUP):
            m = g * GROUP + k
            result = dot(own_band[...], control_own[m]) + dot(side_band[...], control_side[m])
            along[k * rows : (k + 1) * rows, :] = result.astype(BF16)
        along_lat(along, lat_band, smooth)
        running = total[...]
        for k in range(GROUP):
            m = g * GROUP + k
            running = running + perturb_own[m].astype(F32) * smooth[k * rows : k * rows + lon_cells, :]
        total[...] = running
        return carry

    lax.fori_loop(0, groups, forward, 0)

    result = total[...]
    send_sum[0:lon_cells, :] = result.astype(send_sum.dtype)
    send_edge[...] = result[lon_cells - rad :, :].astype(send_edge.dtype)
    sum_copies = []
    for j in range(1, mems):
        sum_copies.append(
            pltpu.make_async_remote_copy(
                send_sum,
                got_sum.at[j - 1],
                sum_send.at[j - 1],
                sum_recv.at[j - 1],
                device_id=(me, lax.rem(mine + j, mems)),
                device_id_type=MESH,
            )
        )
    for j in range(mems):
        for side in range(2):
            sum_copies.append(
                pltpu.make_async_remote_copy(
                    send_sum.at[0:rad] if side == 0 else send_edge,
                    got_edge.at[1 - side, j],
                    edge_send.at[side, j],
                    edge_recv.at[side, j],
                    device_id=(sides[side], lax.rem(mine + j, mems)),
                    device_id_type=MESH,
                )
            )
    for copy in sum_copies:
        copy.start()

    for i in range(1, tiles):
        list_copy(i).wait_recv()
    cells = got_lists[:, 0, 2 * cap : 3 * cap]
    row_of = jnp.floor((cells + 0.5) * (1.0 / lat))
    places[0] = row_of
    places[1] = cells - row_of * lat
    batch = onehot.shape[1] // cap
    field_parts[...] = jnp.zeros_like(field_parts)

    def scatter(s, carry):
        for k in range(batch):
            source = s * batch + k
            values = got_lists[source]
            rows_here = places[0, pl.ds(source, 1), :]
            cols_here = places[1, pl.ds(source, 1), :]
            lanes = slice(k * cap, (k + 1) * cap)
            hit = iota((rows, cap), 0).astype(F32) == rows_here
            for part in range(2):
                value = values[:, part * cap : (part + 1) * cap]
                high = value.astype(BF16).astype(F32)
                rest = value - high
                first = 2 * part * rows
                picked[first : first + rows, lanes] = jnp.where(hit, high, 0.0).astype(BF16)
                picked[first + rows : first + 2 * rows, lanes] = jnp.where(hit, rest, 0.0).astype(BF16)
            base = iota((16, cap), 0).astype(F32)
            for r in range(lat // 16):
                match = (base + float(16 * r)) == cols_here
                onehot[16 * r : 16 * r + 16, lanes] = jnp.where(match, 1.0, 0.0).astype(BF16)
        field_parts[...] += lax.dot_general(
            picked[...], onehot[...], (((1,), (1,)), ((), ())), preferred_element_type=F32
        )
        return carry

    lax.fori_loop(0, tiles // batch, scatter, 0)
    for part in range(2):
        first = 2 * part * rows
        field = field_parts[first : first + lon_cells, :] + field_parts[first + rows : first + rows + lon_cells, :]
        fields[part] = field
        field_edge[0, part] = field[0:rad, :]
        field_edge[1, part] = field[lon_cells - rad :, :]
    field_copies = [
        pltpu.make_async_remote_copy(
            field_edge.at[side],
            got_field.at[1 - side],
            field_send.at[side],
            field_recv.at[side],
            device_id=(sides[side], mine),
            device_id_type=MESH,
        )
        for side in range(2)
    ]
    for copy in field_copies:
        copy.start()

    for copy in sum_copies:
        copy.wait_recv()
    increment = send_sum[0:lon_cells, :].astype(F32)
    for j in range(mems - 1):
        increment = increment + got_sum[j, 0:lon_cells, :].astype(F32)
    spread_own[...] = fields[0] * increment - fields[1]
    for copy in field_copies:
        copy.wait_recv()
    for side in range(2):
        increment = got_edge[side, 0].astype(F32)
        for j in range(1, mems):
            increment = increment + got_edge[side, j].astype(F32)
        spread_side[side * rad : (side + 1) * rad, :] = got_field[side, 0] * increment - got_field[side, 1]

    def finish(g, carry):
        for copy in control_copies(g):
            copy.wait_send()
        for copy in perturb_copies(g):
            copy.wait()
        return carry

    lax.fori_loop(0, groups, finish, 0)
    for i in range(1, tiles):
        list_copy(i).wait_send()
    for copy in sum_copies + field_copies:
        copy.wait_send()


def backward_kernel(
    groups,
    control,
    perturb,
    spread_own,
    spread_side,
    perturb_side,
    own_band,
    side_band,
    lat_band,
    gradient,
    control_own,
    perturb_own,
    side_own,
    along,
    smooth,
    out,
    load_sem,
    out_sem,
):
    members, lon_cells, lat = control_own.shape
    rows = own_band.shape[0]

    def load(g):
        chunk = pl.ds(g * GROUP, GROUP)
        return (
            pltpu.make_async_copy(perturb.at[chunk, 0], perturb_own.at[chunk], load_sem.at[0, g]),
            pltpu.make_async_copy(perturb_side.at[chunk], side_own.at[chunk], load_sem.at[1, g]),
            pltpu.make_async_copy(control.at[chunk, 0], control_own.at[chunk], load_sem.at[2, g]),
        )

    def store(m):
        return pltpu.make_async_copy(out.at[m], gradient.at[m], out_sem.at[m])

    for g in range(groups):
        for copy in load(g):
            copy.start()

    def backward(g, carry):
        for copy in load(g):
            copy.wait()
        for k in range(GROUP):
            m = g * GROUP + k
            own = (perturb_own[m].astype(F32) * spread_own[...]).astype(BF16)
            side = (side_own[m].astype(F32) * spread_side[...]).astype(BF16)
            result = dot(own_band[...], own) + dot(side_band[...], side)
            along[k * rows : (k + 1) * rows, :] = result.astype(BF16)
        along_lat(along, lat_band, smooth)
        for k in range(GROUP):
            m = g * GROUP + k
            value = control_own[m].astype(F32) + smooth[k * rows : k * rows + lon_cells, :]
            out[m] = value[:, None, :]
            store(m).start()
        return carry

    lax.fori_loop(0, groups, backward, 0)

    def finish(m, carry):
        store(m).wait()
        return carry

    lax.fori_loop(0, members, finish, 0)


def local(tiles, mems, control, perturb, lon_taps, lat_taps, innov, inv_var, cell_index, counts):
    members, levels, lon_cells, lat = control.shape
    rad = lon_taps.shape[0] - 1
    cap = innov.shape[2]
    groups = members // GROUP
    rows = (lon_cells + 15) // 16 * 16
    dma = pltpu.SemaphoreType.DMA
    anywhere = pl.BlockSpec(memory_space=pl.ANY)
    inside = pl.BlockSpec(memory_space=pltpu.VMEM)
    batch = 4
    scratch = [
        pltpu.VMEM((members, lon_cells, lat), BF16),
        pltpu.VMEM((members, lon_cells, lat), BF16),
        pltpu.VMEM((members, rad, lat), BF16),
        pltpu.VMEM((members, rad, lat), BF16),
        pltpu.VMEM((members, 2 * rad, lat), BF16),
        pltpu.VMEM((GROUP * rows, lat), BF16),
        pltpu.VMEM((GROUP * rows, lat), F32),
        pltpu.VMEM((lon_cells, lat), F32),
        pltpu.VMEM((rows, lat), SUM_TYPE),
        pltpu.VMEM((rad, lat), SUM_TYPE),
        pltpu.VMEM((mems - 1, rows, lat), SUM_TYPE),
        pltpu.VMEM((2, mems, rad, lat), SUM_TYPE),
        pltpu.VMEM((2, tiles, cap), F32),
        pltpu.VMEM((tiles, 1, 3 * cap), F32),
        pltpu.VMEM((tiles, 1, 3 * cap), F32),
        pltpu.VMEM((lat, batch * cap), BF16),
        pltpu.VMEM((4 * rows, batch * cap), BF16),
        pltpu.VMEM((2, tiles, cap), F32),
        pltpu.VMEM((4 * rows, lat), F32),
        pltpu.VMEM((2, lon_cells, lat), F32),
        pltpu.VMEM((2, 2, rad, lat), F32),
        pltpu.VMEM((2, 2, rad, lat), F32),
        dma((groups + 3,)),
        dma((2, 2, groups)),
        dma((2, 2, groups)),
        dma((tiles,)),
        dma((tiles,)),
        dma((mems - 1,)),
        dma((mems - 1,)),
        dma((2, mems)),
        dma((2, mems)),
        dma((2,)),
        dma((2,)),
    ]
    spread_own, spread_side, perturb_side, own_band, side_band, lat_band = pl.pallas_call(
        functools.partial(forward_kernel, tiles, groups),
        out_shape=(
            jax.ShapeDtypeStruct((lon_cells, lat), F32),
            jax.ShapeDtypeStruct((2 * rad, lat), F32),
            jax.ShapeDtypeStruct((members, 2 * rad, lat), BF16),
            jax.ShapeDtypeStruct((rows, lon_cells), BF16),
            jax.ShapeDtypeStruct((rows, 2 * rad), BF16),
            jax.ShapeDtypeStruct((512, 256), BF16),
        ),
        in_specs=[anywhere, anywhere, inside, inside, anywhere, anywhere, inside, inside],
        out_specs=(inside, inside, anywhere, inside, inside, inside),
        scratch_shapes=scratch,
        compiler_params=pltpu.CompilerParams(
            collective_id=0, has_side_effects=True, vmem_limit_bytes=48 * 2**20
        ),
        name="forward",
    )(control, perturb, lon_taps, lat_taps, innov, inv_var, cell_index, counts)
    gradient = pl.pallas_call(
        functools.partial(backward_kernel, groups),
        out_shape=jax.ShapeDtypeStruct((members, lon_cells, 1, lat), F32),
        in_specs=[anywhere, anywhere, inside, inside, anywhere, inside, inside, inside],
        out_specs=anywhere,
        scratch_shapes=[
            pltpu.VMEM((members, lon_cells, lat), BF16),
            pltpu.VMEM((members, lon_cells, lat), BF16),
            pltpu.VMEM((members, 2 * rad, lat), BF16),
            pltpu.VMEM((GROUP * rows, lat), BF16),
            pltpu.VMEM((GROUP * rows, lat), F32),
            pltpu.VMEM((members, lon_cells, 1, lat), F32),
            dma((3, groups)),
            dma((members,)),
        ],
        compiler_params=pltpu.CompilerParams(vmem_limit_bytes=48 * 2**20),
        name="backward",
    )(control, perturb, spread_own, spread_side, perturb_side, own_band, side_band, lat_band)
    return gradient.reshape(members, levels, lon_cells, lat)


def solution(mesh):
    return jax.shard_map(
        functools.partial(local, mesh.shape["tile"], mesh.shape["mem"]),
        mesh=mesh,
        in_specs=(
            P("mem", None, "tile", None),
            P("mem", None, "tile", None),
            P(),
            P(),
            P("tile", None, None),
            P("tile", None, None),
            P("tile", None, None),
            P("tile", None),
        ),
        out_specs=P("mem", None, "tile", None),
        check_vma=False,
    )
```

```python
import functools

import jax
import jax.numpy as jnp
from jax import lax
from jax.experimental import pallas as pl
from jax.experimental.pallas import tpu as pltpu
from jax.sharding import PartitionSpec as P

MESH = pl.DeviceIdType.MESH
F32 = jnp.float32
BF16 = jnp.bfloat16
GROUP = 5
BACK = 5
AHEAD = 2
PART = 256


def iota(shape, dim):
    return lax.broadcasted_iota(jnp.int32, shape, dim)


def band_block(taps_ref):
    row = taps_ref[...].astype(F32).reshape(1, -1)
    taps = [jnp.broadcast_to(row[:, d : d + 1], (16, 128)) for d in range(row.shape[1])]

    def block(offsets):
        away = jnp.abs(offsets)
        band = jnp.zeros((16, 128), F32)
        for d, tap in enumerate(taps):
            band = jnp.where(away == d, tap, band)
        return band.astype(BF16)

    return block


def build_bands(lon_ref, lat_ref, lon_band, lat_band, lon_cells):
    rad = lon_ref.shape[0] - 1
    rows, depth = lon_band.shape
    row, col = iota((16, 128), 0), iota((16, 128), 1)
    block = band_block(lon_ref)
    side = col - rows
    place = jnp.where(side < rad, side - rad, side - rad + lon_cells)
    place = jnp.where(side < 0, jnp.where(col < lon_cells, col, 4 * rows), place)
    for r in range(0, rows, 16):
        lon_band[r : r + 16, :] = block(row + r - place)[:, 0:depth]
    block = band_block(lat_ref)
    lat_band[...] = jnp.zeros_like(lat_band)
    for r in range(-16, 144, 16):
        piece = block(row + r - col)
        for half in range(2):
            first = 128 + 128 * half + r
            lat_band[first : first + 16, 128 * half : 128 * half + 128] = piece


def dot(a, b):
    return jnp.dot(a, b, preferred_element_type=F32)


def along_lat(along, band):
    windows = [along[:, PART * n : PART * n + 512] for n in range(along.shape[1] // PART - 1)]
    return dot(jnp.concatenate(windows, axis=0), band[...])


def forward_kernel(
    tiles,
    mems,
    groups,
    control,
    perturb,
    lon_taps,
    lat_taps,
    innov,
    inv_var,
    cell_index,
    counts,
    spread,
    perturb_wide,
    lon_band_out,
    lat_band_out,
    lon_band,
    lat_band,
    control_own,
    perturb_own,
    control_low,
    perturb_low,
    control_wide,
    perturb_full,
    along,
    total,
    got_sum,
    part,
    part_low,
    lists,
    cells_here,
    counts_here,
    lon_here,
    lat_here,
    stage,
    got_lists,
    onehot,
    picked,
    places,
    field_parts,
    load_sem,
    keep_sem,
    halo_send,
    halo_recv,
    list_send,
    list_recv,
    sum_send,
    sum_recv,
    part_send,
    part_recv,
    edge_send,
    edge_recv,
):
    me = lax.axis_index("tile")
    mine = lax.axis_index("mem")
    members, lon_cells, lat = control_own.shape
    rows, depth = lon_band.shape
    rad = (depth - rows) // 2
    cap = innov.shape[2]
    upper, lower = slice(rows, rows + rad), slice(rows + rad, depth)
    parts = total.shape[1] // PART
    left, right = lax.rem(me + tiles - 1, tiles), lax.rem(me + 1, tiles)
    sides = (left, right)
    turn = lax.rem(me, 2) * (mems // 2)
    rank = lax.rem(mine + turn, mems)

    loads = [
        pltpu.make_async_copy(
            control.at[pl.ds(g * GROUP, GROUP), 0],
            control_own.at[pl.ds(g * GROUP, GROUP)],
            load_sem.at[g],
        )
        for g in range(groups)
    ]
    others = (
        (inv_var.at[0], lists.at[0]),
        (innov.at[0], lists.at[1]),
        (cell_index.at[0], cells_here),
        (counts, counts_here),
        (perturb.at[:, 0], perturb_own),
        (lon_taps, lon_here),
        (lat_taps, lat_here),
    )
    loads += [
        pltpu.make_async_copy(src, dst, load_sem.at[groups + n]) for n, (src, dst) in enumerate(others)
    ]
    late = groups + 4

    partners = [(tile, mine) for tile in sides]
    partners += [(me, lax.rem(mine + j, mems)) for j in range(1, mems)]
    partners += [(tile, lax.rem(mine + j, mems)) for tile in sides for j in range(1, mems)]
    partners += [(lax.rem(me + i, tiles), mine) for i in range(2, tiles - 1)]
    barrier = pltpu.get_barrier_semaphore()
    for partner in partners:
        pl.semaphore_signal(barrier, inc=1, device_id=partner, device_id_type=MESH)
    for n, load in enumerate(loads):
        if n != late:
            load.start()

    filler = jnp.zeros((rows - lon_cells, lat), F32)

    def stage_edges(own, low, full, start):
        for k in range(GROUP):
            field = own[start + k].astype(F32)
            low[start + k] = field[lon_cells - rad :, :].astype(BF16)
            full[start + k, 0:rows, :] = jnp.concatenate([field, filler], axis=0).astype(BF16)

    def list_copy(i):
        return pltpu.make_async_remote_copy(
            stage.at[lax.rem(me + i, tiles)],
            got_lists.at[i],
            list_send.at[i],
            list_recv.at[i],
            device_id=(lax.rem(me + i, tiles), mine),
            device_id_type=MESH,
        )

    def halo_copies(source, low, wide, kind, g):
        chunk = pl.ds(g * GROUP, GROUP)
        return (
            pltpu.make_async_remote_copy(
                source.at[chunk, 0:rad],
                wide.at[chunk, lower],
                halo_send.at[kind, 0, g],
                halo_recv.at[kind, 0, g],
                device_id=(left, mine),
                device_id_type=MESH,
            ),
            pltpu.make_async_remote_copy(
                low.at[chunk],
                wide.at[chunk, upper],
                halo_send.at[kind, 1, g],
                halo_recv.at[kind, 1, g],
                device_id=(right, mine),
                device_id_type=MESH,
            ),
        )

    def control_copies(g):
        return halo_copies(control_own, control_low, control_wide, 0, g)

    def perturb_copies(g):
        return halo_copies(perturb_own, perturb_low, perturb_wide, 1, g)

    loads[0].wait()
    stage_edges(control_own, control_low, control_wide, 0)
    pl.semaphore_wait(barrier, len(partners))
    for g in range(groups):
        if g > 0:
            loads[g].wait()
            stage_edges(control_own, control_low, control_wide, g * GROUP)
        for copy in control_copies(g):
            copy.start()

    loads[late].start()
    for n, load in enumerate(loads[groups:]):
        if groups + n != late:
            load.wait()
    shape = (tiles, tiles)
    count_row = counts_here[...].astype(F32)
    count_col = jnp.sum(
        jnp.where(iota(shape, 0) == iota(shape, 1), count_row, 0.0), axis=1, keepdims=True
    )
    live = iota((tiles, cap), 1).astype(F32) < count_col
    weight = jnp.where(live, lists[0], 0.0)
    stage[:, 0, 0:cap] = weight
    stage[:, 0, cap : 2 * cap] = weight * lists[1]
    stage[:, 0, 2 * cap : 3 * cap] = cells_here[...].astype(F32)
    for i in range(1, tiles):
        list_copy(i).start()
    got_lists[0] = stage[me]
    loads[late].wait()
    for g in range(groups):
        stage_edges(perturb_own, perturb_low, perturb_full, g * GROUP)
    build_bands(lon_here, lat_here, lon_band, lat_band, lon_cells)
    keeps = [
        pltpu.make_async_copy(src, dst, keep_sem.at[n])
        for n, (src, dst) in enumerate(
            (
                (lon_band, lon_band_out),
                (lat_band, lat_band_out),
                (perturb_full, perturb_wide.at[:, 0:rows]),
            )
        )
    ]
    for keep in keeps:
        keep.start()
    total[...] = jnp.zeros_like(total)
    along[...] = jnp.zeros_like(along)

    def forward(g, carry):
        for copy in control_copies(g):
            copy.wait_recv()
        for copy in perturb_copies(g):
            copy.start()
        for k in range(GROUP):
            result = dot(lon_band[...], control_wide[g * GROUP + k])
            along[k * rows : (k + 1) * rows, 128 : 128 + lat] = result.astype(BF16)
        smooth = along_lat(along, lat_band)
        for n in range(parts):
            lanes = slice(n * PART, min(lat, (n + 1) * PART))
            count = lanes.stop - lanes.start
            running = total[0:lon_cells, lanes]
            for k in range(GROUP):
                first = (n * GROUP + k) * rows
                weight = perturb_own[g * GROUP + k, :, lanes].astype(F32)
                running = running + weight * smooth[first : first + lon_cells, 0:count]
            total[0:lon_cells, lanes] = running
        return carry

    lax.fori_loop(0, groups, forward, 0)

    def lanes_of(q):
        return pl.ds(pl.multiple_of(jnp.minimum(q, parts - 1) * PART, PART), PART)

    def sum_copy(j):
        return pltpu.make_async_remote_copy(
            total.at[:, lanes_of(lax.rem(rank + j, mems))],
            got_sum.at[j - 1],
            sum_send.at[j - 1],
            sum_recv.at[j - 1],
            device_id=(me, lax.rem(mine + j, mems)),
            device_id_type=MESH,
        )

    def if_owner(owner, action):
        @pl.when(owner < parts)
        def _():
            action()

    for j in range(1, mems):
        if_owner(lax.rem(rank + j, mems), sum_copy(j).start)

    for i in range(1, tiles):
        list_copy(i).wait_recv()
    cells = got_lists[:, 0, 2 * cap : 3 * cap]
    row_of = jnp.floor((cells + 0.5) * (1.0 / lat))
    col_of = cells - row_of * lat - rank.astype(F32) * PART
    places[0] = row_of
    places[1] = jnp.where((col_of >= 0) & (col_of < PART), col_of, -1.0)
    batch = onehot.shape[1] // cap
    field_parts[...] = jnp.zeros_like(field_parts)
    row_base = iota((16, cap), 0).astype(F32).astype(BF16)
    one = jnp.ones((16, cap), BF16)
    nothing = jnp.zeros((16, cap), BF16)

    def wide(row):
        return jnp.broadcast_to(row, (16, cap)).astype(BF16)

    def scatter(s, carry):
        for k in range(batch):
            source = s * batch + k
            values = got_lists[source]
            lanes = slice(k * cap, (k + 1) * cap)
            row_at = wide(places[0, pl.ds(source, 1), :])
            col_at = wide(places[1, pl.ds(source, 1), :])
            for kind in range(2):
                value = values[:, kind * cap : (kind + 1) * cap]
                rest = wide(value - value.astype(BF16).astype(F32))
                high = wide(value)
                first = 2 * kind * rows
                for r in range(0, rows, 16):
                    match = row_base == row_at - r
                    picked[first + r : first + r + 16, lanes] = jnp.where(match, high, nothing)
                    picked[first + rows + r : first + rows + r + 16, lanes] = jnp.where(match, rest, nothing)
            for r in range(0, PART, 16):
                match = row_base == col_at - r
                onehot[r : r + 16, lanes] = jnp.where(match, one, nothing)
        field_parts[...] += lax.dot_general(
            picked[...], onehot[...], (((1,), (1,)), ((), ())), preferred_element_type=F32
        )
        return carry

    lax.fori_loop(0, tiles // batch, scatter, 0)
    fields = [
        field_parts[2 * kind * rows : (2 * kind + 1) * rows, :]
        + field_parts[(2 * kind + 1) * rows : (2 * kind + 2) * rows, :]
        for kind in range(2)
    ]

    def part_copy(j):
        return pltpu.make_async_remote_copy(
            part,
            spread.at[0:rows, lanes_of(rank)],
            part_send.at[j - 1],
            part_recv.at[rank],
            device_id=(me, lax.rem(mine + j, mems)),
            device_id_type=MESH,
        )

    def edge_copy(side, j):
        return pltpu.make_async_remote_copy(
            part.at[0:rad] if side == 0 else part_low,
            spread.at[lower if side == 0 else upper, lanes_of(rank)],
            edge_send.at[side, j],
            edge_recv.at[side, rank],
            device_id=(sides[side], lax.rem(mine + j, mems)),
            device_id_type=MESH,
        )

    def own_copy():
        return pltpu.make_async_copy(part, spread.at[0:rows, lanes_of(rank)], keep_sem.at[len(keeps)])

    @pl.when(rank < parts)
    def _():
        for j in range(1, mems):
            sum_copy(j).wait_recv()
        increment = total[:, lanes_of(rank)]
        for j in range(mems - 1):
            increment = increment + got_sum[j]
        result = fields[0] * increment - fields[1]
        part[...] = result
        part_low[...] = result[lon_cells - rad : lon_cells, :]
        for j in range(1, mems):
            edge_copy(0, j).start()
            edge_copy(1, j).start()
        for j in range(1, mems):
            part_copy(j).start()
        edge_copy(0, 0).start()
        edge_copy(1, 0).start()
        own_copy().start()

    def finish(g, carry):
        for copy in control_copies(g):
            copy.wait_send()
        for copy in perturb_copies(g):
            copy.wait()
        return carry

    lax.fori_loop(0, groups, finish, 0)
    for i in range(1, tiles):
        list_copy(i).wait_send()
    for keep in keeps:
        keep.wait()
    for j in range(1, mems):
        if_owner(lax.rem(rank + j, mems), sum_copy(j).wait_send)

    def got_part(p):
        return pltpu.make_async_remote_copy(
            part,
            spread.at[0:rows, p * PART : (p + 1) * PART],
            part_send.at[0],
            part_recv.at[p],
            device_id=(me, lax.rem(mine + 1, mems)),
            device_id_type=MESH,
        )

    def got_edge(side, p):
        return pltpu.make_async_remote_copy(
            part_low,
            spread.at[lower if side == 0 else upper, p * PART : (p + 1) * PART],
            edge_send.at[side, 0],
            edge_recv.at[side, p],
            device_id=(sides[side], mine),
            device_id_type=MESH,
        )

    for p in range(parts):

        @pl.when(rank != p)
        def _(p=p):
            got_part(p).wait_recv()

        for side in range(2):
            got_edge(side, p).wait_recv()

    @pl.when(rank < parts)
    def _():
        own_copy().wait()
        for j in range(1, mems):
            part_copy(j).wait_send()
        for j in range(mems):
            for side in range(2):
                edge_copy(side, j).wait_send()


def backward_kernel(
    groups,
    control,
    spread_in,
    perturb_wide,
    lon_band_in,
    lat_band_in,
    gradient,
    control_own,
    perturb_own,
    spread,
    lon_band,
    lat_band,
    along,
    out,
    first_sem,
    load_sem,
    out_sem,
):
    members, lon_cells, lat = control_own.shape
    rows = lon_band.shape[0]
    parts = spread.shape[1] // PART

    def load(g):
        chunk = pl.ds(g * BACK, BACK)
        return (
            pltpu.make_async_copy(perturb_wide.at[chunk], perturb_own.at[chunk], load_sem.at[0, g]),
            pltpu.make_async_copy(control.at[chunk, 0], control_own.at[chunk], load_sem.at[1, g]),
        )

    def store(m):
        return pltpu.make_async_copy(out.at[m], gradient.at[m], out_sem.at[m])

    pairs = ((spread_in, spread), (lon_band_in, lon_band), (lat_band_in, lat_band))
    firsts = [pltpu.make_async_copy(src, dst, first_sem.at[n]) for n, (src, dst) in enumerate(pairs)]
    load(0)[0].start()
    for copy in firsts:
        copy.start()
    load(0)[1].start()
    for g in range(1, AHEAD):
        for copy in load(g):
            copy.start()
    along[...] = jnp.zeros_like(along)
    for copy in firsts:
        copy.wait()

    def backward(g, carry):
        for copy in load(g):
            copy.wait()

        @pl.when(g + AHEAD < groups)
        def _():
            for copy in load(g + AHEAD):
                copy.start()

        for k in range(BACK):
            product = (perturb_own[g * BACK + k].astype(F32) * spread[:, 0:lat]).astype(BF16)
            result = dot(lon_band[...], product)
            along[k * rows : (k + 1) * rows, 128 : 128 + lat] = result.astype(BF16)
        smooth = along_lat(along, lat_band)
        for k in range(BACK):
            m = g * BACK + k
            for n in range(parts):
                lanes = slice(n * PART, min(lat, (n + 1) * PART))
                count = lanes.stop - lanes.start
                first = (n * BACK + k) * rows
                value = control_own[m, :, lanes].astype(F32) + smooth[first : first + lon_cells, 0:count]
                out[m, :, :, lanes] = value[:, None, :]
            store(m).start()
        return carry

    lax.fori_loop(0, groups, backward, 0)

    def finish(m, carry):
        store(m).wait()
        return carry

    lax.fori_loop(0, members, finish, 0)


def local(tiles, mems, control, perturb, lon_taps, lat_taps, innov, inv_var, cell_index, counts):
    members, levels, lon_cells, lat = control.shape
    rad = lon_taps.shape[0] - 1
    cap = innov.shape[2]
    groups = members // GROUP
    rows = (lon_cells + 15) // 16 * 16
    dma = pltpu.SemaphoreType.DMA
    anywhere = pl.BlockSpec(memory_space=pl.ANY)
    batch = 4
    width = (lat + PART - 1) // PART * PART
    depth = rows + 2 * rad
    bands = [pltpu.VMEM((rows, depth), BF16), pltpu.VMEM((512, PART), BF16)]
    scratch = bands + [
        pltpu.VMEM((members, lon_cells, lat), BF16),
        pltpu.VMEM((members, lon_cells, lat), BF16),
        pltpu.VMEM((members, rad, lat), BF16),
        pltpu.VMEM((members, rad, lat), BF16),
        pltpu.VMEM((members, depth, lat), BF16),
        pltpu.VMEM((members, rows, lat), BF16),
        pltpu.VMEM((GROUP * rows, width + PART), BF16),
        pltpu.VMEM((rows, width), F32),
        pltpu.VMEM((mems - 1, rows, PART), F32),
        pltpu.VMEM((rows, PART), F32),
        pltpu.VMEM((rad, PART), F32),
        pltpu.VMEM((2, tiles, cap), F32),
        pltpu.VMEM((tiles, cap), jnp.int32),
        pltpu.VMEM(counts.shape, jnp.int32),
        pltpu.VMEM(lon_taps.shape, BF16),
        pltpu.VMEM(lat_taps.shape, BF16),
        pltpu.VMEM((tiles, 1, 3 * cap), F32),
        pltpu.VMEM((tiles, 1, 3 * cap), F32),
        pltpu.VMEM((PART, batch * cap), BF16),
        pltpu.VMEM((4 * rows, batch * cap), BF16),
        pltpu.VMEM((2, tiles, cap), F32),
        pltpu.VMEM((4 * rows, PART), F32),
        dma((groups + 7,)),
        dma((4,)),
        dma((2, 2, groups)),
        dma((2, 2, groups)),
        dma((tiles,)),
        dma((tiles,)),
        dma((mems - 1,)),
        dma((mems - 1,)),
        dma((mems - 1,)),
        dma((mems,)),
        dma((2, mems)),
        dma((2, mems)),
    ]
    middle = pl.pallas_call(
        functools.partial(forward_kernel, tiles, mems, groups),
        out_shape=(
            jax.ShapeDtypeStruct((depth, width), F32),
            jax.ShapeDtypeStruct((members, depth, lat), BF16),
            jax.ShapeDtypeStruct((rows, depth), BF16),
            jax.ShapeDtypeStruct((512, PART), BF16),
        ),
        in_specs=[anywhere] * 8,
        out_specs=(anywhere,) * 4,
        scratch_shapes=scratch,
        compiler_params=pltpu.CompilerParams(
            collective_id=0, has_side_effects=True, vmem_limit_bytes=63 * 2**20
        ),
        name="forward",
    )(control, perturb, lon_taps, lat_taps, innov, inv_var, cell_index, counts)
    gradient = pl.pallas_call(
        functools.partial(backward_kernel, members // BACK),
        out_shape=jax.ShapeDtypeStruct((members, lon_cells, 1, lat), F32),
        in_specs=[anywhere] * 5,
        out_specs=anywhere,
        scratch_shapes=[
            pltpu.VMEM((members, lon_cells, lat), BF16),
            pltpu.VMEM((members, depth, lat), BF16),
            pltpu.VMEM((depth, width), F32),
            *bands,
            pltpu.VMEM((BACK * rows, width + PART), BF16),
            pltpu.VMEM((members, lon_cells, 1, lat), F32),
            dma((3,)),
            dma((2, members // BACK)),
            dma((members,)),
        ],
        compiler_params=pltpu.CompilerParams(vmem_limit_bytes=63 * 2**20),
        name="backward",
    )(control, *middle)
    return gradient.reshape(members, levels, lon_cells, lat)


def solution(mesh):
    return jax.shard_map(
        functools.partial(local, mesh.shape["tile"], mesh.shape["mem"]),
        mesh=mesh,
        in_specs=(
            P("mem", None, "tile", None),
            P("mem", None, "tile", None),
            P(),
            P(),
            P("tile", None, None),
            P("tile", None, None),
            P("tile", None, None),
            P("tile", None),
        ),
        out_specs=P("mem", None, "tile", None),
        check_vma=False,
    )
```

```python
import functools

import jax
import jax.numpy as jnp
from jax import lax
from jax.experimental import pallas as pl
from jax.experimental.pallas import tpu as pltpu
from jax.sharding import PartitionSpec as P

MESH = pl.DeviceIdType.MESH
F32 = jnp.float32
BF16 = jnp.bfloat16
GROUP = 5
BACK = 5
AHEAD = 2
PART = 256


def iota(shape, dim):
    return lax.broadcasted_iota(jnp.int32, shape, dim)


def band_block(taps_ref):
    row = taps_ref[...].astype(F32).reshape(1, -1)
    taps = [jnp.broadcast_to(row[:, d : d + 1], (16, 128)) for d in range(row.shape[1])]

    def block(offsets):
        away = jnp.abs(offsets)
        band = jnp.zeros((16, 128), F32)
        for d, tap in enumerate(taps):
            band = jnp.where(away == d, tap, band)
        return band.astype(BF16)

    return block


def build_bands(lon_ref, lat_ref, lon_band, lat_band, lon_cells):
    rad = lon_ref.shape[0] - 1
    rows, depth = lon_band.shape
    row, col = iota((16, 128), 0), iota((16, 128), 1)
    block = band_block(lon_ref)
    side = col - rows
    place = jnp.where(side < rad, side - rad, side - rad + lon_cells)
    place = jnp.where(side < 0, jnp.where(col < lon_cells, col, 4 * rows), place)
    for r in range(0, rows, 16):
        lon_band[r : r + 16, :] = block(row + r - place)[:, 0:depth]
    block = band_block(lat_ref)
    lat_band[...] = jnp.zeros_like(lat_band)
    for r in range(-16, 144, 16):
        piece = block(row + r - col)
        for half in range(2):
            first = 128 + 128 * half + r
            lat_band[first : first + 16, 128 * half : 128 * half + 128] = piece


def dot(a, b):
    return jnp.dot(a, b, preferred_element_type=F32)


def along_lat(along, band):
    windows = [along[:, PART * n : PART * n + 512] for n in range(along.shape[1] // PART - 1)]
    return dot(jnp.concatenate(windows, axis=0), band[...])


def forward_kernel(
    tiles,
    mems,
    groups,
    control,
    perturb,
    lon_taps,
    lat_taps,
    innov,
    inv_var,
    cell_index,
    counts,
    spread,
    perturb_wide,
    lon_band_out,
    lat_band_out,
    lon_band,
    lat_band,
    control_own,
    perturb_own,
    control_low,
    perturb_low,
    control_wide,
    perturb_full,
    along,
    total,
    got_sum,
    part,
    part_low,
    lists,
    cells_here,
    counts_here,
    lon_here,
    lat_here,
    stage,
    got_lists,
    onehot,
    picked,
    places,
    field_parts,
    load_sem,
    keep_sem,
    halo_send,
    halo_recv,
    list_send,
    list_recv,
    sum_send,
    sum_recv,
    part_send,
    part_recv,
    edge_send,
    edge_recv,
):
    me = lax.axis_index("tile")
    mine = lax.axis_index("mem")
    members, lon_cells, lat = control_own.shape
    rows, depth = lon_band.shape
    rad = (depth - rows) // 2
    cap = innov.shape[2]
    upper, lower = slice(rows, rows + rad), slice(rows + rad, depth)
    parts = total.shape[1] // PART
    left, right = lax.rem(me + tiles - 1, tiles), lax.rem(me + 1, tiles)
    sides = (left, right)
    turn = lax.rem(me, 2) * (mems // 2)
    rank = lax.rem(mine + turn, mems)

    loads = [
        pltpu.make_async_copy(
            control.at[pl.ds(g * GROUP, GROUP), 0],
            control_own.at[pl.ds(g * GROUP, GROUP)],
            load_sem.at[g],
        )
        for g in range(groups)
    ]
    others = (
        (inv_var.at[0], lists.at[0]),
        (innov.at[0], lists.at[1]),
        (cell_index.at[0], cells_here),
        (counts, counts_here),
        (perturb.at[:, 0], perturb_own),
        (lon_taps, lon_here),
        (lat_taps, lat_here),
    )
    loads += [
        pltpu.make_async_copy(src, dst, load_sem.at[groups + n]) for n, (src, dst) in enumerate(others)
    ]
    late = groups + 4

    partners = [(tile, mine) for tile in sides]
    partners += [(me, lax.rem(mine + j, mems)) for j in range(1, mems)]
    partners += [(tile, lax.rem(mine + j, mems)) for tile in sides for j in range(1, mems)]
    partners += [(lax.rem(me + i, tiles), mine) for i in range(2, tiles - 1)]
    barrier = pltpu.get_barrier_semaphore()
    for partner in partners:
        pl.semaphore_signal(barrier, inc=1, device_id=partner, device_id_type=MESH)
    for n, load in enumerate(loads):
        if n != late:
            load.start()

    filler = jnp.zeros((rows - lon_cells, lat), F32)

    def stage_edges(own, low, full, start):
        for k in range(GROUP):
            field = own[start + k].astype(F32)
            low[start + k] = field[lon_cells - rad :, :].astype(BF16)
            full[start + k, 0:rows, :] = jnp.concatenate([field, filler], axis=0).astype(BF16)

    def list_copy(i):
        return pltpu.make_async_remote_copy(
            stage.at[lax.rem(me + i, tiles)],
            got_lists.at[i],
            list_send.at[i],
            list_recv.at[i],
            device_id=(lax.rem(me + i, tiles), mine),
            device_id_type=MESH,
        )

    def halo_copies(source, low, wide, kind, g):
        chunk = pl.ds(g * GROUP, GROUP)
        return (
            pltpu.make_async_remote_copy(
                source.at[chunk, 0:rad],
                wide.at[chunk, lower],
                halo_send.at[kind, 0, g],
                halo_recv.at[kind, 0, g],
                device_id=(left, mine),
                device_id_type=MESH,
            ),
            pltpu.make_async_remote_copy(
                low.at[chunk],
                wide.at[chunk, upper],
                halo_send.at[kind, 1, g],
                halo_recv.at[kind, 1, g],
                device_id=(right, mine),
                device_id_type=MESH,
            ),
        )

    def control_copies(g):
        return halo_copies(control_own, control_low, control_wide, 0, g)

    def perturb_copies(g):
        return halo_copies(perturb_own, perturb_low, perturb_wide, 1, g)

    loads[0].wait()
    stage_edges(control_own, control_low, control_wide, 0)
    pl.semaphore_wait(barrier, len(partners))
    for g in range(groups):
        if g > 0:
            loads[g].wait()
            stage_edges(control_own, control_low, control_wide, g * GROUP)
        for copy in control_copies(g):
            copy.start()

    loads[late].start()
    for n, load in enumerate(loads[groups:]):
        if groups + n != late:
            load.wait()
    shape = (tiles, tiles)
    count_row = counts_here[...].astype(F32)
    count_col = jnp.sum(
        jnp.where(iota(shape, 0) == iota(shape, 1), count_row, 0.0), axis=1, keepdims=True
    )
    live = iota((tiles, cap), 1).astype(F32) < count_col
    weight = jnp.where(live, lists[0], 0.0)
    stage[:, 0, 0:cap] = weight
    stage[:, 0, cap : 2 * cap] = weight * lists[1]
    stage[:, 0, 2 * cap : 3 * cap] = cells_here[...].astype(F32)
    for i in range(1, tiles):
        list_copy(i).start()
    got_lists[0] = stage[me]
    loads[late].wait()
    for g in range(groups):
        stage_edges(perturb_own, perturb_low, perturb_full, g * GROUP)
    build_bands(lon_here, lat_here, lon_band, lat_band, lon_cells)
    keeps = [
        pltpu.make_async_copy(src, dst, keep_sem.at[n])
        for n, (src, dst) in enumerate(
            (
                (lon_band, lon_band_out),
                (lat_band, lat_band_out),
                (perturb_full, perturb_wide.at[:, 0:rows]),
            )
        )
    ]
    for keep in keeps:
        keep.start()
    total[...] = jnp.zeros_like(total)
    along[...] = jnp.zeros_like(along)

    def forward(g, carry):
        for copy in control_copies(g):
            copy.wait_recv()
        for copy in perturb_copies(g):
            copy.start()
        for k in range(GROUP):
            result = dot(lon_band[...], control_wide[g * GROUP + k])
            along[k * rows : (k + 1) * rows, 128 : 128 + lat] = result.astype(BF16)
        smooth = along_lat(along, lat_band)
        for n in range(parts):
            lanes = slice(n * PART, min(lat, (n + 1) * PART))
            count = lanes.stop - lanes.start
            running = total[0:lon_cells, lanes]
            for k in range(GROUP):
                first = (n * GROUP + k) * rows
                weight = perturb_own[g * GROUP + k, :, lanes].astype(F32)
                running = running + weight * smooth[first : first + lon_cells, 0:count]
            total[0:lon_cells, lanes] = running
        return carry

    lax.fori_loop(0, groups, forward, 0)

    def lanes_of(q):
        return pl.ds(pl.multiple_of(jnp.minimum(q, parts - 1) * PART, PART), PART)

    def sum_copy(j):
        return pltpu.make_async_remote_copy(
            total.at[:, lanes_of(lax.rem(rank + j, mems))],
            got_sum.at[j - 1],
            sum_send.at[j - 1],
            sum_recv.at[j - 1],
            device_id=(me, lax.rem(mine + j, mems)),
            device_id_type=MESH,
        )

    def if_owner(owner, action):
        @pl.when(owner < parts)
        def _():
            action()

    for j in range(1, mems):
        if_owner(lax.rem(rank + j, mems), sum_copy(j).start)

    for i in range(1, tiles):
        list_copy(i).wait_recv()
    cells = got_lists[:, 0, 2 * cap : 3 * cap]
    row_of = jnp.floor((cells + 0.5) * (1.0 / lat))
    col_of = cells - row_of * lat - rank.astype(F32) * PART
    places[0] = row_of
    places[1] = jnp.where((col_of >= 0) & (col_of < PART), col_of, -1.0)
    batch = onehot.shape[1] // cap
    field_parts[...] = jnp.zeros_like(field_parts)
    row_base = iota((16, cap), 0).astype(F32).astype(BF16)
    one = jnp.ones((16, cap), BF16)
    nothing = jnp.zeros((16, cap), BF16)

    def wide(row):
        return jnp.broadcast_to(row, (16, cap)).astype(BF16)

    def scatter(s, carry):
        for k in range(batch):
            source = s * batch + k
            values = got_lists[source]
            lanes = slice(k * cap, (k + 1) * cap)
            row_at = wide(places[0, pl.ds(source, 1), :])
            col_at = wide(places[1, pl.ds(source, 1), :])
            for kind in range(2):
                value = values[:, kind * cap : (kind + 1) * cap]
                rest = wide(value - value.astype(BF16).astype(F32))
                high = wide(value)
                first = 2 * kind * rows
                for r in range(0, rows, 16):
                    match = row_base == row_at - r
                    picked[first + r : first + r + 16, lanes] = jnp.where(match, high, nothing)
                    picked[first + rows + r : first + rows + r + 16, lanes] = jnp.where(match, rest, nothing)
            for r in range(0, PART, 16):
                match = row_base == col_at - r
                onehot[r : r + 16, lanes] = jnp.where(match, one, nothing)
        field_parts[...] += lax.dot_general(
            picked[...], onehot[...], (((1,), (1,)), ((), ())), preferred_element_type=F32
        )
        return carry

    lax.fori_loop(0, tiles // batch, scatter, 0)
    fields = [
        field_parts[2 * kind * rows : (2 * kind + 1) * rows, :]
        + field_parts[(2 * kind + 1) * rows : (2 * kind + 2) * rows, :]
        for kind in range(2)
    ]

    def part_copy(j):
        return pltpu.make_async_remote_copy(
            part,
            spread.at[0:rows, lanes_of(rank)],
            part_send.at[j - 1],
            part_recv.at[rank],
            device_id=(me, lax.rem(mine + j, mems)),
            device_id_type=MESH,
        )

    def edge_copy(side, j):
        return pltpu.make_async_remote_copy(
            part.at[0:rad] if side == 0 else part_low,
            spread.at[lower if side == 0 else upper, lanes_of(rank)],
            edge_send.at[side, j],
            edge_recv.at[side, rank],
            device_id=(sides[side], lax.rem(mine + j, mems)),
            device_id_type=MESH,
        )

    def own_copy():
        return pltpu.make_async_copy(part, spread.at[0:rows, lanes_of(rank)], keep_sem.at[len(keeps)])

    @pl.when(rank < parts)
    def _():
        for j in range(1, mems):
            sum_copy(j).wait_recv()
        increment = total[:, lanes_of(rank)]
        for j in range(mems - 1):
            increment = increment + got_sum[j]
        result = fields[0] * increment - fields[1]
        part[...] = result
        part_low[...] = result[lon_cells - rad : lon_cells, :]
        for j in range(1, mems):
            edge_copy(0, j).start()
            edge_copy(1, j).start()
        for j in range(1, mems):
            part_copy(j).start()
        edge_copy(0, 0).start()
        edge_copy(1, 0).start()
        own_copy().start()

    def finish(g, carry):
        for copy in control_copies(g):
            copy.wait_send()
        for copy in perturb_copies(g):
            copy.wait()
        return carry

    lax.fori_loop(0, groups, finish, 0)
    for i in range(1, tiles):
        list_copy(i).wait_send()
    for keep in keeps:
        keep.wait()
    for j in range(1, mems):
        if_owner(lax.rem(rank + j, mems), sum_copy(j).wait_send)

    def got_part(p):
        return pltpu.make_async_remote_copy(
            part,
            spread.at[0:rows, p * PART : (p + 1) * PART],
            part_send.at[0],
            part_recv.at[p],
            device_id=(me, lax.rem(mine + 1, mems)),
            device_id_type=MESH,
        )

    def got_edge(side, p):
        return pltpu.make_async_remote_copy(
            part_low,
            spread.at[lower if side == 0 else upper, p * PART : (p + 1) * PART],
            edge_send.at[side, 0],
            edge_recv.at[side, p],
            device_id=(sides[side], mine),
            device_id_type=MESH,
        )

    for p in range(parts):

        @pl.when(rank != p)
        def _(p=p):
            got_part(p).wait_recv()

        for side in range(2):
            got_edge(side, p).wait_recv()

    @pl.when(rank < parts)
    def _():
        own_copy().wait()
        for j in range(1, mems):
            part_copy(j).wait_send()
        for j in range(mems):
            for side in range(2):
                edge_copy(side, j).wait_send()


def backward_kernel(
    groups,
    control,
    spread_in,
    perturb_wide,
    lon_band_in,
    lat_band_in,
    gradient,
    control_own,
    perturb_own,
    spread,
    lon_band,
    lat_band,
    along,
    out,
    first_sem,
    load_sem,
    out_sem,
):
    members, lon_cells, lat = control_own.shape
    rows = lon_band.shape[0]
    parts = spread.shape[1] // PART

    def load(g):
        chunk = pl.ds(g * BACK, BACK)
        return (
            pltpu.make_async_copy(perturb_wide.at[chunk], perturb_own.at[chunk], load_sem.at[0, g]),
            pltpu.make_async_copy(control.at[chunk, 0], control_own.at[chunk], load_sem.at[1, g]),
        )

    def store(m):
        return pltpu.make_async_copy(out.at[m, 0:lon_cells], gradient.at[m], out_sem.at[m])

    pairs = ((spread_in, spread), (lon_band_in, lon_band), (lat_band_in, lat_band))
    firsts = [pltpu.make_async_copy(src, dst, first_sem.at[n]) for n, (src, dst) in enumerate(pairs)]
    load(0)[0].start()
    for copy in firsts:
        copy.start()
    load(0)[1].start()
    for g in range(1, AHEAD):
        for copy in load(g):
            copy.start()
    along[...] = jnp.zeros_like(along)
    for copy in firsts:
        copy.wait()

    def backward(g, carry):
        for copy in load(g):
            copy.wait()

        @pl.when(g + AHEAD < groups)
        def _():
            for copy in load(g + AHEAD):
                copy.start()

        for k in range(BACK):
            product = (perturb_own[g * BACK + k].astype(F32) * spread[:, 0:lat]).astype(BF16)
            result = dot(lon_band[...], product)
            along[k * rows : (k + 1) * rows, 128 : 128 + lat] = result.astype(BF16)
        smooth = along_lat(along, lat_band)
        for k in range(BACK):
            m = g * BACK + k
            for n in range(parts):
                lanes = slice(n * PART, min(lat, (n + 1) * PART))
                count = lanes.stop - lanes.start
                first = (n * BACK + k) * rows
                value = control_own[m, :, lanes].astype(F32) + smooth[first : first + lon_cells, 0:count]
                out[m, 0:lon_cells, :, lanes] = value[:, None, :]
            store(m).start()
        return carry

    lax.fori_loop(0, groups, backward, 0)

    def finish(m, carry):
        store(m).wait()
        return carry

    lax.fori_loop(0, members, finish, 0)


def local(tiles, mems, control, perturb, lon_taps, lat_taps, innov, inv_var, cell_index, counts):
    members, levels, lon_cells, lat = control.shape
    rad = lon_taps.shape[0] - 1
    cap = innov.shape[2]
    groups = members // GROUP
    rows = (lon_cells + 15) // 16 * 16
    dma = pltpu.SemaphoreType.DMA
    anywhere = pl.BlockSpec(memory_space=pl.ANY)
    batch = 4
    width = (lat + PART - 1) // PART * PART
    depth = rows + 2 * rad
    bands = [pltpu.VMEM((rows, depth), BF16), pltpu.VMEM((512, PART), BF16)]
    scratch = bands + [
        pltpu.VMEM((members, lon_cells, lat), BF16),
        pltpu.VMEM((members, lon_cells, lat), BF16),
        pltpu.VMEM((members, rad, lat), BF16),
        pltpu.VMEM((members, rad, lat), BF16),
        pltpu.VMEM((members, depth, lat), BF16),
        pltpu.VMEM((members, rows, lat), BF16),
        pltpu.VMEM((GROUP * rows, width + PART), BF16),
        pltpu.VMEM((rows, width), F32),
        pltpu.VMEM((mems - 1, rows, PART), F32),
        pltpu.VMEM((rows, PART), F32),
        pltpu.VMEM((rad, PART), F32),
        pltpu.VMEM((2, tiles, cap), F32),
        pltpu.VMEM((tiles, cap), jnp.int32),
        pltpu.VMEM(counts.shape, jnp.int32),
        pltpu.VMEM(lon_taps.shape, BF16),
        pltpu.VMEM(lat_taps.shape, BF16),
        pltpu.VMEM((tiles, 1, 3 * cap), F32),
        pltpu.VMEM((tiles, 1, 3 * cap), F32),
        pltpu.VMEM((PART, batch * cap), BF16),
        pltpu.VMEM((4 * rows, batch * cap), BF16),
        pltpu.VMEM((2, tiles, cap), F32),
        pltpu.VMEM((4 * rows, PART), F32),
        dma((groups + 7,)),
        dma((4,)),
        dma((2, 2, groups)),
        dma((2, 2, groups)),
        dma((tiles,)),
        dma((tiles,)),
        dma((mems - 1,)),
        dma((mems - 1,)),
        dma((mems - 1,)),
        dma((mems,)),
        dma((2, mems)),
        dma((2, mems)),
    ]
    middle = pl.pallas_call(
        functools.partial(forward_kernel, tiles, mems, groups),
        out_shape=(
            jax.ShapeDtypeStruct((depth, width), F32),
            jax.ShapeDtypeStruct((members, depth, lat), BF16),
            jax.ShapeDtypeStruct((rows, depth), BF16),
            jax.ShapeDtypeStruct((512, PART), BF16),
        ),
        in_specs=[anywhere] * 8,
        out_specs=(anywhere,) * 4,
        scratch_shapes=scratch,
        compiler_params=pltpu.CompilerParams(
            collective_id=0, has_side_effects=True, vmem_limit_bytes=63 * 2**20
        ),
        name="forward",
    )(control, perturb, lon_taps, lat_taps, innov, inv_var, cell_index, counts)
    gradient = pl.pallas_call(
        functools.partial(backward_kernel, members // BACK),
        out_shape=jax.ShapeDtypeStruct((members, lon_cells, 1, lat), F32),
        in_specs=[anywhere] * 5,
        out_specs=anywhere,
        scratch_shapes=[
            pltpu.VMEM((members, lon_cells, lat), BF16),
            pltpu.VMEM((members, depth, lat), BF16),
            pltpu.VMEM((depth, width), F32),
            *bands,
            pltpu.VMEM((BACK * rows, width + PART), BF16),
            pltpu.VMEM((members, rows, 1, lat), F32),
            dma((3,)),
            dma((2, members // BACK)),
            dma((members,)),
        ],
        compiler_params=pltpu.CompilerParams(vmem_limit_bytes=63 * 2**20),
        name="backward",
    )(control, *middle)
    return gradient.reshape(members, levels, lon_cells, lat)


def solution(mesh):
    return jax.shard_map(
        functools.partial(local, mesh.shape["tile"], mesh.shape["mem"]),
        mesh=mesh,
        in_specs=(
            P("mem", None, "tile", None),
            P("mem", None, "tile", None),
            P(),
            P(),
            P("tile", None, None),
            P("tile", None, None),
            P("tile", None, None),
            P("tile", None),
        ),
        out_specs=P("mem", None, "tile", None),
        check_vma=False,
    )
```
